32 devices in a mesh: gx: 4 (over z), gy: 2 (over y), gz: 4 (over x, core).
Axes of the slice: x: 2, y: 2, z: 4, core: 2. Of those that a mesh axis runs over, the one named last changes fastest.
Arguments:
- grad_out: bfloat16 [64, 32, 16, 64], P(None, 'gx', 'gy', 'gz'), may hold values from -6 to 6
- features: bfloat16 [64, 32, 16, 64], P(None, 'gx', 'gy', 'gz'), may hold values from -6 to 6
- brick_mask: int32 [4, 2, 8], P('gx', 'gy', 'gz'), may hold values 0 or 1
- voxel_mask: int32 [32, 16, 64], P('gx', 'gy', 'gz'), may hold values 0 or 1
- weight: bfloat16 [64, 1728], replicated, may hold values from -0.15625 to 0.15625
Outputs:
- grad_input: bfloat16 [64, 32, 16, 64], P(None, 'gx', 'gy', 'gz')
- grad_weight: float32 [64, 1728], replicated
The draws below stay inside these ranges and needn't reach their ends.
All inputs are finite; a program needn't handle non-finite values. No bound on the sum of `brick_mask` or of `voxel_mask` on one device may be relied on, other than what follows from the above.
Results may differ from the reference program's by a relative error of at most 0.001.
Values may be sent and summed in bfloat16 or wider, within the bound.
A program may use at most 64 MiB of HBM per device.

```python
import math
import jax
import jax.numpy as jnp
from jax import lax

CH = 64
BRICK = 8
NX = 32
NY = 16
NZ = 64
NBX = 4
NBY = 2
NBZ = 8


def place_ends(values, key, least, top_value):
    longest = values.shape.index(max(values.shape))
    spots = []
    for shift in (0, 1):
        where = [jax.random.randint(jax.random.fold_in(key, axis), (), 0, length) for axis, length in enumerate(values.shape)]
        where[longest] = (where[longest] + shift) % values.shape[longest]
        spots.append(tuple(where))
    return values.at[spots[0]].set(least).at[spots[1]].set(top_value)


def shard_levels(rng, dims, cuts, low, high):
    level, own = 1.0, jax.random.fold_in(rng, 6)
    for dim, shards_of in cuts:
        draws = jnp.exp(jax.random.uniform(jax.random.fold_in(own, dim), (shards_of,), jnp.float32, low / len(cuts), high / len(cuts)))
        level = level * jnp.repeat(draws, dims[dim] // shards_of).reshape([-1 if axis == dim else 1 for axis in range(len(dims))])
    return level


def noise(key, dims, scale, bound, split=(), held_as=jnp.bfloat16):
    factor_of = shard_levels(key, dims, split, -0.22, 0.18) if split else 1.0
    values = jax.random.normal(key, dims, jnp.float32) * scale * factor_of
    return jnp.minimum(jnp.maximum(values, -bound), bound).astype(held_as)


def setup_inputs(seed: int = 0) -> dict:
    splits = jax.random.split(jax.random.key(seed), 6)
    grad_out = noise(splits[0], (CH, NX, NY, NZ), 1.0, 6.0, ((1, 4), (2, 2), (3, 4)))
    features = noise(splits[1], (CH, NX, NY, NZ), 1.0, 6.0, ((1, 4), (2, 2), (3, 4)))
    brick_mask = place_ends((jax.random.randint(splits[2], (NBX, NBY, NBZ), 0, 4) < 3).astype(jnp.int32), jax.random.fold_in(splits[2], 1), 0, 1)
    voxel_mask = place_ends((jax.random.randint(splits[3], (NX, NY, NZ), 0, 5) < 3).astype(jnp.int32), jax.random.fold_in(splits[3], 1), 0, 1)
    weight = noise(splits[4], (CH, 27 * CH), (27 * CH) ** -0.5, 0.15625)
    return {"grad_out": grad_out, "features": features, "brick_mask": brick_mask, "voxel_mask": voxel_mask, "weight": weight}


def reference(grad_out, features, brick_mask, voxel_mask, weight):
    upsampled = jnp.repeat(jnp.repeat(jnp.repeat(brick_mask, BRICK, 0), BRICK, 1), BRICK, 2)
    active = upsampled * voxel_mask > 0
    masked_grad = jnp.where(active[None], grad_out, jnp.zeros_like(grad_out))
    masked_feat = jnp.where(active[None], features, jnp.zeros_like(features))
    padded = jnp.pad(masked_grad, ((0, 0), (1, 1), (1, 1), (1, 1)))
    count = NX * NY * NZ
    feat_flat = masked_feat.reshape(CH, count)
    total = jnp.zeros((CH, count), jnp.float32)
    blocks = []
    for shift_x in (-1, 0, 1):
        for shift_y in (-1, 0, 1):
            for shift_z in (-1, 0, 1):
                index = 9 * (shift_x + 1) + 3 * (shift_y + 1) + (shift_z + 1)
                shifted = padded[:, 1 - shift_x:1 - shift_x + NX, 1 - shift_y:1 - shift_y + NY, 1 - shift_z:1 - shift_z + NZ]
                shifted = shifted.reshape(CH, count)
                kernel = weight[:, index * CH:(index + 1) * CH]
                total = total + jnp.dot(kernel, shifted, preferred_element_type=jnp.float32)
                blocks.append(lax.dot_general(feat_flat, shifted, (((1,), (1,)), ((), ())), preferred_element_type=jnp.float32))
    grad_input = jnp.where(active.reshape(1, count), total, jnp.zeros_like(total)).astype(jnp.bfloat16)
    grad_weight = jnp.concatenate(blocks, axis=1) * (1.0 / math.sqrt(count))
    return (grad_input.reshape(CH, NX, NY, NZ), grad_weight)
```

```python
import functools
import math

import jax
import jax.numpy as jnp
from jax import lax
from jax.experimental import pallas as pl
from jax.experimental.pallas import tpu as pltpu
from jax.sharding import PartitionSpec as P

BRICK = 8
MESH = pl.DeviceIdType.MESH
F32, BF16 = jnp.float32, jnp.bfloat16


def ceil_div(a, b):
    return -(-a // b)


def plan(n_gx, n_gy, n_gz, chans):
    cores = 2 if n_gz % 2 == 0 else 1
    plane = n_gy * (n_gz // cores)
    tiles = 27 * chans * chans // 1024
    part2 = ceil_div(ceil_div(tiles, cores), plane)
    part1 = part2 * plane
    part3 = ceil_div(part2, n_gx)
    return cores, plane, tiles, part1, part2, part3


def iota(shape, dim):
    return lax.broadcasted_iota(jnp.int32, shape, dim)


def kernel(
    sizes, scale, g_ref, f_ref, b_ref, v_ref, w_ref, gi_ref, gw_ref,
    pad, cols, mask, faces, rims, terms, in1, in2, sum2, in3, out3, full,
    halo_send, halo_recv, core_send, core_recv, plane_send, plane_recv, line_send, line_recv,
):
    n_gx, n_gy, n_gz = sizes
    sx, sy, sz, chans = g_ref.shape
    nxy, count = sx * sy, sx * sy * sz
    cores, plane, tiles, part1, part2, part3 = plan(n_gx, n_gy, n_gz, chans)
    gx, gy, gz = lax.axis_index("gx"), lax.axis_index("gy"), lax.axis_index("gz")
    core, xh = lax.rem(gz, cores), gz // cores
    wide = n_gz // cores
    spot = gy * wide + xh

    def plane_peer(step):
        other = lax.rem(spot + step, plane)
        return (gx, other // wide, lax.rem(other, wide) * cores + core)

    def line_peer(step):
        return (lax.rem(gx + step, n_gx), gy, gz)

    core_peer = (gx, gy, xh * cores + (cores - 1 - core))
    partners = [plane_peer(s) for s in range(1, plane)] + [line_peer(s) for s in range(1, n_gx)]
    if cores == 2:
        partners.append(core_peer)
    if n_gz > cores:
        partners.append((gx, gy, lax.rem(gz + n_gz + 2 * core - 1, n_gz)))
    barrier = pltpu.get_barrier_semaphore()
    for partner in partners:
        pl.semaphore_signal(barrier, inc=1, device_id=partner, device_id_type=MESH)

    bricks = jnp.zeros((sx, sy, sz), jnp.int32)
    at = [iota((sx, sy, sz), d) // BRICK for d in range(3)]
    for i in range(b_ref.shape[0]):
        for j in range(b_ref.shape[1]):
            for l in range(b_ref.shape[2]):
                here = (at[0] == i) & (at[1] == j) & (at[2] == l)
                bricks = jnp.where(here, b_ref[i, j, l], bricks)
    active = jnp.where(bricks * v_ref[...] > 0, 1.0, 0.0).reshape(nxy, sz).astype(BF16)
    own = jnp.where(iota((count, nxy), 0) // sz == iota((count, nxy), 1), 1.0, 0.0).astype(BF16)
    spread = jnp.dot(own, active, preferred_element_type=F32)
    level = lax.rem(iota((count, sz), 0), sz) == iota((count, sz), 1)
    spread = jnp.where(level, spread, 0.0).astype(BF16)
    lit = jnp.dot(spread, jnp.ones((sz, chans), BF16), preferred_element_type=F32)
    mask[...] = lit
    lit = lit.astype(BF16)
    grad = g_ref[...].reshape(count, chans) * lit

    row, col = iota((2 * nxy, count), 0), iota((2 * nxy, count), 1)
    pick = jnp.where(row < nxy, row * sz, (row - nxy) * sz + sz - 1) == col
    pick = jnp.where(pick, 1.0, 0.0).astype(BF16)
    ends = jnp.dot(pick, grad, preferred_element_type=F32)
    zeros = jnp.zeros((2 * nxy, chans), F32)
    faces[...] = jnp.concatenate([zeros, ends], axis=1).astype(BF16)

    pl.semaphore_wait(barrier, len(partners))

    def swap(base, index, length, device, low_src, high_src, low_dst, high_dst):
        def down():
            return pltpu.make_async_remote_copy(
                src_ref=low_src, dst_ref=high_dst, send_sem=halo_send.at[base],
                recv_sem=halo_recv.at[base], device_id=device(lax.rem(index + length - 1, length)),
                device_id_type=MESH,
            )

        def up():
            return pltpu.make_async_remote_copy(
                src_ref=high_src, dst_ref=low_dst, send_sem=halo_send.at[base + 1],
                recv_sem=halo_recv.at[base + 1], device_id=device(lax.rem(index + 1, length)),
                device_id_type=MESH,
            )

        if length > 1:
            @pl.when(index > 0)
            def _():
                down().start()

            @pl.when(index < length - 1)
            def _():
                up().start()

        def finish():
            @pl.when(index == 0)
            def _():
                low_dst[...] = jnp.zeros(low_dst.shape, low_dst.dtype)

            @pl.when(index == length - 1)
            def _():
                high_dst[...] = jnp.zeros(high_dst.shape, high_dst.dtype)

            if length > 1:
                @pl.when(index > 0)
                def _():
                    up().wait_recv()
                    down().wait_send()

                @pl.when(index < length - 1)
                def _():
                    down().wait_recv()
                    up().wait_send()

        return finish

    def columns(tile):
        lead = tile.shape[:-2]
        rows = math.prod(tile.shape[:-1])
        wide_tile = tile.reshape(rows, 2 * chans).astype(F32)
        after = pltpu.roll(wide_tile, rows - 1, 0)
        before = pltpu.roll(wide_tile, 1, 0)
        other = pltpu.roll(wide_tile, chans, 1)
        z, lane = lax.rem(iota(wide_tile.shape, 0), sz), iota(wide_tile.shape, 1)
        first = jnp.where((lane < chans) & (z != sz - 1), after, other)
        second = jnp.where(z == 0, other, before)
        both = jnp.concatenate([first, second], axis=1).astype(BF16)
        return both.reshape(*lead, sz, 4 * chans)

    finish = swap(
        0, gz, n_gz, lambda i: (gx, gy, i),
        faces.at[pl.ds(0, nxy)], faces.at[pl.ds(nxy, nxy)],
        rims.at[pl.ds(0, nxy)], rims.at[pl.ds(nxy, nxy)],
    )
    feat = (f_ref[...].reshape(count, chans) * lit).astype(F32).T.astype(BF16)
    finish()
    row, col = iota((count, 2 * nxy), 0), iota((count, 2 * nxy), 1)
    place = jnp.where(col < nxy, col * sz, (col - nxy) * sz + sz - 1) == row
    place = jnp.where(place, 1.0, 0.0).astype(BF16)
    rim = jnp.dot(place, rims[...], preferred_element_type=F32)
    body = jnp.concatenate([grad.astype(F32), jnp.zeros((count, chans), F32)], axis=1) + rim
    pad[1 : sx + 1, 1 : sy + 1] = body.astype(BF16).reshape(sx, sy, sz, 2 * chans)

    inner = pl.ds(1, sy)
    finish = swap(
        2, gx, n_gx, lambda i: (i, gy, gz),
        pad.at[1, inner], pad.at[sx, inner], pad.at[0, inner], pad.at[sx + 1, inner],
    )
    cols[1 : sx + 1, 1 : sy + 1] = columns(pad[1 : sx + 1, 1 : sy + 1])
    finish()
    finish = swap(
        4, gy, n_gy, lambda i: (gx, i, gz),
        pad.at[:, 1], pad.at[:, sy], pad.at[:, 0], pad.at[:, sy + 1],
    )
    cols[0, 1 : sy + 1] = columns(pad[0, 1 : sy + 1])
    cols[sx + 1, 1 : sy + 1] = columns(pad[sx + 1, 1 : sy + 1])

    half = chans // 2
    per = half // 8

    def shifted(a, b):
        return cols[1 - a : 1 - a + sx, 1 - b : 1 - b + sy].reshape(count, 4 * chans)

    def weight_term(a, b):
        got = jnp.dot(feat, shifted(a, b), preferred_element_type=F32)
        low = iota((half, 2 * chans), 1) < chans
        for e in range(3):
            tile = e // 2
            top = got[:half, tile * 2 * chans : (tile + 1) * 2 * chans]
            end = got[half:, tile * 2 * chans : (tile + 1) * 2 * chans]
            if e % 2 == 0:
                both = jnp.where(low, top, pltpu.roll(end, chans, 1))
            else:
                both = jnp.where(low, pltpu.roll(top, chans, 1), end)
            k = 9 * (a + 1) + 3 * (b + 1) + e
            terms[k * per : (k + 1) * per] = both.reshape(per, 8, 2 * chans)

    for a in (-1, 0, 1):
        weight_term(a, 0)
    if cores * part1 > tiles:
        terms[tiles:] = jnp.zeros((cores * part1 - tiles, 8, 2 * chans), F32)
    finish()
    cols[:, 0] = columns(pad[:, 0])
    cols[:, sy + 1] = columns(pad[:, sy + 1])
    for a in (-1, 0, 1):
        weight_term(a, -1)
        weight_term(a, 1)

    def send(src, dst, send_sem, recv_sem, device):
        copy = pltpu.make_async_remote_copy(
            src_ref=src, dst_ref=dst, send_sem=send_sem, recv_sem=recv_sem,
            device_id=device, device_id_type=MESH,
        )
        copy.start()
        return copy

    flights = []
    base1 = core * part1
    if cores == 2:
        flights = [send(terms.at[pl.ds((1 - core) * part1, part1)], in1, core_send.at[0],
                        core_recv.at[0], core_peer)]

    def input_rows(x):
        wide_cols, kernels = [], []
        for a in (-1, 0, 1):
            for b in (-1, 0, 1):
                rows = cols[x + 1 - a, 1 - b : 1 - b + sy].reshape(sy * sz, 4 * chans)
                k = 9 * (a + 1) + 3 * (b + 1)
                wide_cols.append(rows[:, : 3 * chans])
                kernels.append(w_ref[:, k * chans : (k + 3) * chans])
        total = jnp.zeros((sy * sz, chans), F32)
        for rows, kern in zip(wide_cols, kernels):
            total = total + lax.dot_general(
                rows, kern, (((1,), (1,)), ((), ())), preferred_element_type=F32
            )
        keep = mask[x * sy * sz : (x + 1) * sy * sz] > 0
        gi_ref[x] = jnp.where(keep, total, 0.0).astype(BF16).reshape(sy, sz, chans)

    for x in range(sx // 2):
        input_rows(x)
    mine = pl.ds(base1, part1)
    for copy in flights:
        copy.wait()
        terms[mine] = terms[mine] + in1[...]
    flights = []
    for step in range(1, plane):
        other = lax.rem(spot + step, plane)
        flights.append(send(
            terms.at[pl.ds(base1 + other * part2, part2)], in2.at[step - 1],
            plane_send.at[step - 1], plane_recv.at[step - 1], plane_peer(step),
        ))
    for x in range(sx // 2, sx):
        input_rows(x)
    acc = terms[pl.ds(base1 + spot * part2, part2)]
    for step, copy in enumerate(flights):
        copy.wait()
        acc = acc + in2[step]
    sum2[:part2] = acc
    if n_gx * part3 > part2:
        sum2[part2:] = jnp.zeros((n_gx * part3 - part2, 8, 2 * chans), F32)
    flights = []
    for step in range(1, n_gx):
        other = lax.rem(gx + step, n_gx)
        flights.append(send(
            sum2.at[pl.ds(other * part3, part3)], in3.at[step - 1],
            line_send.at[step - 1], line_recv.at[step - 1], line_peer(step),
        ))
    acc = sum2[pl.ds(gx * part3, part3)]
    for step, copy in enumerate(flights):
        copy.wait()
        acc = acc + in3[step]

    out3[pl.ds(gx * part3, part3)] = acc * scale
    flights = []
    for step in range(1, n_gx):
        here = out3.at[pl.ds(gx * part3, part3)]
        slot = n_gx - 1 + step - 1
        flights.append(send(here, here, line_send.at[slot], line_recv.at[slot], line_peer(step)))
    for copy in flights:
        copy.wait()
    flights = []
    here = pl.ds(base1 + spot * part2, part2)
    for step in range(1, plane):
        slot = plane - 1 + step - 1
        flights.append(send(
            out3.at[pl.ds(0, part2)], full.at[here],
            plane_send.at[slot], plane_recv.at[slot], plane_peer(step),
        ))
    full[here] = out3[:part2]
    for copy in flights:
        copy.wait()
    if cores == 2:
        send(full.at[mine], full.at[mine], core_send.at[1], core_recv.at[1], core_peer).wait()

    low = iota((half, 2 * chans), 1) < chans
    for k in range(0, 27, 2):
        one = full[k * per : (k + 1) * per].reshape(half, 2 * chans)
        if k == 26:
            gw_ref[:half, k * chans :] = one[:, :chans]
            gw_ref[half:, k * chans :] = pltpu.roll(one, chans, 1)[:, :chans]
            continue
        two = full[(k + 1) * per : (k + 2) * per].reshape(half, 2 * chans)
        at_k = slice(k * chans, (k + 2) * chans)
        gw_ref[:half, at_k] = jnp.where(low, one, pltpu.roll(two, chans, 1))
        gw_ref[half:, at_k] = jnp.where(low, pltpu.roll(one, chans, 1), two)


def local(sizes, grad_out, features, brick_mask, voxel_mask, weight):
    chans, sx, sy, sz = grad_out.shape
    n_gx, n_gy, n_gz = sizes
    cores, plane, tiles, part1, part2, part3 = plan(n_gx, n_gy, n_gz, chans)
    scale = 1.0 / math.sqrt(sx * sy * sz * n_gx * n_gy * n_gz)
    vmem = pl.BlockSpec(memory_space=pltpu.VMEM)
    dma = lambda n: pltpu.SemaphoreType.DMA((max(n, 1),))
    tile = (8, 2 * chans)
    grad_input, grad_weight = pl.pallas_call(
        functools.partial(kernel, sizes, scale),
        out_shape=(
            jax.ShapeDtypeStruct((sx, sy, sz, chans), BF16),
            jax.ShapeDtypeStruct((chans, 27 * chans), F32),
        ),
        in_specs=[vmem, vmem, pl.BlockSpec(memory_space=pltpu.SMEM), vmem, vmem],
        out_specs=(vmem, vmem),
        scratch_shapes=[
            pltpu.VMEM((sx + 2, sy + 2, sz, 2 * chans), BF16),
            pltpu.VMEM((sx + 2, sy + 2, sz, 4 * chans), BF16),
            pltpu.VMEM((sx * sy * sz, chans), F32),
            pltpu.VMEM((2 * sx * sy, 2 * chans), BF16),
            pltpu.VMEM((2 * sx * sy, 2 * chans), BF16),
            pltpu.VMEM((cores * part1, *tile), F32),
            pltpu.VMEM((part1, *tile), F32),
            pltpu.VMEM((max(plane - 1, 1), part2, *tile), F32),
            pltpu.VMEM((n_gx * part3, *tile), F32),
            pltpu.VMEM((max(n_gx - 1, 1), part3, *tile), F32),
            pltpu.VMEM((n_gx * part3, *tile), F32),
            pltpu.VMEM((cores * part1, *tile), F32),
            dma(6), dma(6), dma(2), dma(2),
            dma(2 * (plane - 1)), dma(2 * (plane - 1)),
            dma(2 * (n_gx - 1)), dma(2 * (n_gx - 1)),
        ],
        compiler_params=pltpu.CompilerParams(
            collective_id=0, has_side_effects=True, vmem_limit_bytes=40 * 1024 * 1024
        ),
    )(
        jnp.transpose(grad_out, (1, 2, 3, 0)),
        jnp.transpose(features, (1, 2, 3, 0)),
        brick_mask,
        voxel_mask,
        weight,
    )
    return jnp.transpose(grad_input, (3, 0, 1, 2)), grad_weight


def solution(mesh):
    sizes = tuple(mesh.shape[name] for name in ("gx", "gy", "gz"))
    return jax.shard_map(
        functools.partial(local, sizes),
        mesh=mesh,
        in_specs=(
            P(None, "gx", "gy", "gz"),
            P(None, "gx", "gy", "gz"),
            P("gx", "gy", "gz"),
            P("gx", "gy", "gz"),
            P(),
        ),
        out_specs=(P(None, "gx", "gy", "gz"), P()),
        check_vma=False,
    )
```

```python
import functools
import math

import jax
import jax.numpy as jnp
from jax import lax
from jax.experimental import pallas as pl
from jax.experimental.pallas import tpu as pltpu
from jax.sharding import PartitionSpec as P

BRICK = 8
MESH = pl.DeviceIdType.MESH
F32, BF16 = jnp.float32, jnp.bfloat16


def ceil_div(a, b):
    return -(-a // b)


def plan(sizes, chans):
    n_gx, n_gy, n_gz = sizes
    cores = 2 if n_gz % 2 == 0 else 1
    plane = n_gy * (n_gz // cores)
    tiles = 9 * chans * chans // 1024
    streams = []
    for count, order in ((tiles, (cores, n_gx, plane)), (2 * tiles, (cores, plane, n_gx))):
        stages, left = [], count
        for peers in order:
            left = ceil_div(left, peers)
            stages.append((peers, left))
        streams.append((count, stages))
    return cores, plane, streams


def div(x, n):
    return lax.shift_right_logical(x, n.bit_length() - 1) if n & (n - 1) == 0 else x // n


def mod(x, n):
    return x & (n - 1) if n & (n - 1) == 0 else lax.rem(x, n)


def iota(shape, dim):
    return lax.broadcasted_iota(jnp.int32, shape, dim)


def kernel(
    sizes, scale, g_hbm, f_hbm, b_hbm, v_hbm, w_hbm, gi_ref, gw_ref,
    g_ref, f_ref, b_ref, v_ref, w_ref, load_sem,
    pad, cols, mask, faces, rims, halo_send, halo_recv, *stream_refs,
):
    n_gx, n_gy, n_gz = sizes
    sx, sy, sz, chans = g_ref.shape
    nxy, count = sx * sy, sx * sy * sz
    cores, plane, streams = plan(sizes, chans)
    loads = [
        pltpu.make_async_copy(src, dst, load_sem.at[i])
        for i, (src, dst) in enumerate(
            [(b_hbm, b_ref), (v_hbm, v_ref), (g_hbm, g_ref), (f_hbm, f_ref), (w_hbm, w_ref)]
        )
    ]
    for load in loads:
        load.start()
    gx, gy, gz = lax.axis_index("gx"), lax.axis_index("gy"), lax.axis_index("gz")
    core, xh = lax.rem(gz, cores), gz // cores
    wide = n_gz // cores
    spot = gy * wide + xh

    def plane_peer(step):
        other = lax.rem(spot + step, plane)
        return (gx, other // wide, lax.rem(other, wide) * cores + core)

    def line_peer(step):
        return (lax.rem(gx + step, n_gx), gy, gz)

    def core_peer(step):
        return (gx, gy, xh * cores + lax.rem(core + step, cores))

    partners = [plane_peer(s) for s in range(1, plane)] + [line_peer(s) for s in range(1, n_gx)]
    if cores == 2:
        partners.append(core_peer(1))
    if n_gz > cores:
        partners.append((gx, gy, lax.rem(gz + n_gz + 2 * core - 1, n_gz)))
    barrier = pltpu.get_barrier_semaphore()
    for partner in partners:
        pl.semaphore_signal(barrier, inc=1, device_id=partner, device_id_type=MESH)

    bricks = jnp.zeros((sx, sy, sz), jnp.int32)
    loads[0].wait()
    loads[1].wait()
    at = [div(iota((sx, sy, sz), d), BRICK) for d in range(3)]
    for i in range(b_ref.shape[0]):
        for j in range(b_ref.shape[1]):
            for l in range(b_ref.shape[2]):
                here = (at[0] == i) & (at[1] == j) & (at[2] == l)
                bricks = jnp.where(here, b_ref[i, j, l], bricks)
    active = jnp.where(bricks * v_ref[...] > 0, 1.0, 0.0).reshape(nxy, sz).astype(BF16)
    own = jnp.where(div(iota((count, nxy), 0), sz) == iota((count, nxy), 1), 1.0, 0.0).astype(BF16)
    spread = jnp.dot(own, active, preferred_element_type=F32)
    level = mod(iota((count, sz), 0), sz) == iota((count, sz), 1)
    spread = jnp.where(level, spread, 0.0).astype(BF16)
    lit = jnp.dot(spread, jnp.ones((sz, chans), BF16), preferred_element_type=F32)
    mask[...] = lit
    lit = lit.astype(BF16)
    loads[2].wait()
    grad = g_ref[...].reshape(count, chans) * lit

    row, col = iota((2 * nxy, count), 0), iota((2 * nxy, count), 1)
    pick = jnp.where(row < nxy, row * sz, (row - nxy) * sz + sz - 1) == col
    pick = jnp.where(pick, 1.0, 0.0).astype(BF16)
    ends = jnp.dot(pick, grad, preferred_element_type=F32)
    zeros = jnp.zeros((2 * nxy, chans), F32)
    faces[...] = jnp.concatenate([zeros, ends], axis=1).astype(BF16)

    pl.semaphore_wait(barrier, len(partners))

    def swap(base, index, length, device, low_src, high_src, low_dst, high_dst):
        def down():
            return pltpu.make_async_remote_copy(
                src_ref=low_src, dst_ref=high_dst, send_sem=halo_send.at[base],
                recv_sem=halo_recv.at[base], device_id=device(lax.rem(index + length - 1, length)),
                device_id_type=MESH,
            )

        def up():
            return pltpu.make_async_remote_copy(
                src_ref=high_src, dst_ref=low_dst, send_sem=halo_send.at[base + 1],
                recv_sem=halo_recv.at[base + 1], device_id=device(lax.rem(index + 1, length)),
                device_id_type=MESH,
            )

        if length > 1:
            @pl.when(index > 0)
            def _():
                down().start()

            @pl.when(index < length - 1)
            def _():
                up().start()

        def finish():
            @pl.when(index == 0)
            def _():
                low_dst[...] = jnp.zeros(low_dst.shape, low_dst.dtype)

            @pl.when(index == length - 1)
            def _():
                high_dst[...] = jnp.zeros(high_dst.shape, high_dst.dtype)

            if length > 1:
                @pl.when(index > 0)
                def _():
                    up().wait_recv()
                    down().wait_send()

                @pl.when(index < length - 1)
                def _():
                    down().wait_recv()
                    up().wait_send()

        return finish

    def columns(tile):
        lead = tile.shape[:-2]
        rows = math.prod(tile.shape[:-1])
        wide_tile = tile.reshape(rows, 2 * chans).astype(F32)
        after = pltpu.roll(wide_tile, rows - 1, 0)
        before = pltpu.roll(wide_tile, 1, 0)
        other = pltpu.roll(wide_tile, chans, 1)
        z, lane = mod(iota(wide_tile.shape, 0), sz), iota(wide_tile.shape, 1)
        first = jnp.where((lane < chans) & (z != sz - 1), after, other)
        second = jnp.where(z == 0, other, before)
        both = jnp.concatenate([first, second], axis=1).astype(BF16)
        return both.reshape(*lead, sz, 4 * chans)

    finish = swap(
        0, gz, n_gz, lambda i: (gx, gy, i),
        faces.at[pl.ds(0, nxy)], faces.at[pl.ds(nxy, nxy)],
        rims.at[pl.ds(0, nxy)], rims.at[pl.ds(nxy, nxy)],
    )
    loads[3].wait()
    feat = (f_ref[...].reshape(count, chans) * lit).astype(F32).T.astype(BF16)
    finish()
    row, col = iota((count, 2 * nxy), 0), iota((count, 2 * nxy), 1)
    place = jnp.where(col < nxy, col * sz, (col - nxy) * sz + sz - 1) == row
    place = jnp.where(place, 1.0, 0.0).astype(BF16)
    rim = jnp.dot(place, rims[...], preferred_element_type=F32)
    body = jnp.concatenate([grad.astype(F32), jnp.zeros((count, chans), F32)], axis=1) + rim
    pad[1 : sx + 1, 1 : sy + 1] = body.astype(BF16).reshape(sx, sy, sz, 2 * chans)

    inner = pl.ds(1, sy)
    finish = swap(
        2, gx, n_gx, lambda i: (i, gy, gz),
        pad.at[1, inner], pad.at[sx, inner], pad.at[0, inner], pad.at[sx + 1, inner],
    )
    cols[1 : sx + 1, 1 : sy + 1] = columns(pad[1 : sx + 1, 1 : sy + 1])
    finish()
    finish = swap(
        4, gy, n_gy, lambda i: (gx, i, gz),
        pad.at[:, 1], pad.at[:, sy], pad.at[:, 0], pad.at[:, sy + 1],
    )
    cols[0, 1 : sy + 1] = columns(pad[0, 1 : sy + 1])
    cols[sx + 1, 1 : sy + 1] = columns(pad[sx + 1, 1 : sy + 1])

    half = chans // 2
    per = half // 8

    def shifted(a, b):
        return cols[1 - a : 1 - a + sx, 1 - b : 1 - b + sy].reshape(count, 4 * chans)

    def weight_term(a, b, terms, first):
        got = jnp.dot(feat, shifted(a, b), preferred_element_type=F32)
        low = iota((half, 2 * chans), 1) < chans
        for e in range(3):
            tile = e // 2
            top = got[:half, tile * 2 * chans : (tile + 1) * 2 * chans]
            end = got[half:, tile * 2 * chans : (tile + 1) * 2 * chans]
            if e % 2 == 0:
                both = jnp.where(low, top, pltpu.roll(end, chans, 1))
            else:
                both = jnp.where(low, pltpu.roll(top, chans, 1), end)
            at_tile = (first + e) * per
            terms[at_tile : at_tile + per] = both.reshape(per, 8, 2 * chans)

    class Stream:
        def __init__(self, which):
            self.tiles, self.stages = streams[which]
            refs = stream_refs[which * 15 : (which + 1) * 15]
            self.sums, self.ins, self.outs = refs[0:3], refs[3:6], refs[6:9]
            self.sends, self.recvs = refs[9:12], refs[12:15]
            across, along = (spot, plane_peer), (gx, line_peer)
            self.who = [(core, core_peer)] + ([along, across] if which == 0 else [across, along])
            self.flights = []

        def fly(self, level, slot, src, dst, step):
            copy = pltpu.make_async_remote_copy(
                src_ref=src, dst_ref=dst, send_sem=self.sends[level].at[slot],
                recv_sem=self.recvs[level].at[slot], device_id=self.who[level][1](step),
                device_id_type=MESH,
            )
            copy.start()
            self.flights.append(copy)

        def fill(self, level, used):
            peers, share = self.stages[level]
            if peers * share > used:
                self.sums[level][used:] = jnp.zeros((peers * share - used, 8, 2 * chans), F32)

        def give(self, level):
            peers, share = self.stages[level]
            for step in range(1, peers):
                other = lax.rem(self.who[level][0] + step, peers)
                self.fly(level, step - 1, self.sums[level].at[pl.ds(other * share, share)],
                         self.ins[level].at[step - 1], step)

        def take(self, level):
            peers, share = self.stages[level]
            acc = self.sums[level][pl.ds(self.who[level][0] * share, share)]
            for step, copy in enumerate(self.flights):
                copy.wait()
                acc = acc + self.ins[level][step]
            self.flights = []
            if level < 2:
                self.sums[level + 1][:share] = acc
                self.fill(level + 1, share)
            else:
                self.outs[2][pl.ds(self.who[2][0] * share, share)] = acc * scale

        def give_back(self, level):
            peers, share = self.stages[level]
            here = pl.ds(self.who[level][0] * share, share)
            src = self.outs[level].at[here] if level == 2 else self.outs[level + 1].at[pl.ds(0, share)]
            for step in range(1, peers):
                self.fly(level, peers + step - 2, src, self.outs[level].at[here], step)
            if level < 2:
                self.outs[level][here] = self.outs[level + 1][:share]

        def take_back(self):
            for copy in self.flights:
                copy.wait()
            self.flights = []

    early, late = Stream(0), Stream(1)
    for a in (-1, 0, 1):
        weight_term(a, 0, early.sums[0], 3 * (a + 1))
    early.fill(0, early.tiles)
    early.give(0)
    finish()
    cols[:, 0] = columns(pad[:, 0])
    cols[:, sy + 1] = columns(pad[:, sy + 1])
    for a in (-1, 0, 1):
        weight_term(a, -1, late.sums[0], 3 * (a + 1))
    early.take(0)
    early.give(1)
    for a in (-1, 0, 1):
        weight_term(a, 1, late.sums[0], 9 + 3 * (a + 1))
    late.fill(0, late.tiles)
    late.give(0)

    def input_rows(x):
        wide_cols, kernels = [], []
        for a in (-1, 0, 1):
            for b in (-1, 0, 1):
                rows = cols[x + 1 - a, 1 - b : 1 - b + sy].reshape(sy * sz, 4 * chans)
                k = 9 * (a + 1) + 3 * (b + 1)
                wide_cols.append(rows[:, : 3 * chans])
                kernels.append(w_ref[:, k * chans : (k + 3) * chans])
        total = jnp.zeros((sy * sz, chans), F32)
        for rows, kern in zip(wide_cols, kernels):
            total = total + lax.dot_general(
                rows, kern, (((1,), (1,)), ((), ())), preferred_element_type=F32
            )
        keep = mask[x * sy * sz : (x + 1) * sy * sz] > 0
        gi_ref[x] = jnp.where(keep, total, 0.0).astype(BF16).reshape(sy, sz, chans)

    loads[4].wait()
    late.take(0)
    late.give(1)
    for x in range(sx // 2):
        input_rows(x)
    early.take(1)
    early.give(2)
    for x in range(sx // 2, sx):
        input_rows(x)
    late.take(1)
    late.give(2)
    early.take(2)
    early.give_back(2)
    late.take(2)
    late.give_back(2)
    early.take_back()
    early.give_back(1)
    late.take_back()
    late.give_back(1)
    early.take_back()
    early.give_back(0)
    late.take_back()
    late.give_back(0)
    early.take_back()
    late.take_back()

    def block(k):
        a, b, e = k // 9, k // 3 % 3, k % 3
        full = early.outs[0] if b == 1 else late.outs[0]
        place = (0 if b < 2 else 9) + 3 * a + e
        return full[place * per : (place + 1) * per].reshape(half, 2 * chans)

    low = iota((half, 2 * chans), 1) < chans
    for k in range(0, 27, 2):
        one = block(k)
        if k == 26:
            gw_ref[:half, k * chans :] = one[:, :chans]
            gw_ref[half:, k * chans :] = pltpu.roll(one, chans, 1)[:, :chans]
            continue
        two = block(k + 1)
        at_k = slice(k * chans, (k + 2) * chans)
        gw_ref[:half, at_k] = jnp.where(low, one, pltpu.roll(two, chans, 1))
        gw_ref[half:, at_k] = jnp.where(low, pltpu.roll(one, chans, 1), two)


def local(sizes, grad_out, features, brick_mask, voxel_mask, weight):
    chans, sx, sy, sz = grad_out.shape
    n_gx, n_gy, n_gz = sizes
    cores, plane, streams = plan(sizes, chans)
    scale = 1.0 / math.sqrt(sx * sy * sz * n_gx * n_gy * n_gz)
    vmem = pl.BlockSpec(memory_space=pltpu.VMEM)
    dma = lambda n: pltpu.SemaphoreType.DMA((max(n, 1),))
    hbm = pl.BlockSpec(memory_space=pltpu.HBM)
    tile = (8, 2 * chans)
    stream_refs = []
    for _, stages in streams:
        whole = [pltpu.VMEM((peers * share, *tile), F32) for peers, share in stages]
        ins = [pltpu.VMEM((max(peers - 1, 1), share, *tile), F32) for peers, share in stages]
        sems = [dma(2 * (peers - 1)) for peers, _ in stages]
        stream_refs += whole + ins + whole + sems + sems
    grad_input, grad_weight = pl.pallas_call(
        functools.partial(kernel, sizes, scale),
        out_shape=(
            jax.ShapeDtypeStruct((sx, sy, sz, chans), BF16),
            jax.ShapeDtypeStruct((chans, 27 * chans), F32),
        ),
        in_specs=[hbm] * 5,
        out_specs=(vmem, vmem),
        scratch_shapes=[
            pltpu.VMEM((sx, sy, sz, chans), BF16),
            pltpu.VMEM((sx, sy, sz, chans), BF16),
            pltpu.SMEM(brick_mask.shape, jnp.int32),
            pltpu.VMEM((sx, sy, sz), jnp.int32),
            pltpu.VMEM(weight.shape, BF16),
            dma(5),
            pltpu.VMEM((sx + 2, sy + 2, sz, 2 * chans), BF16),
            pltpu.VMEM((sx + 2, sy + 2, sz, 4 * chans), BF16),
            pltpu.VMEM((sx * sy * sz, chans), F32),
            pltpu.VMEM((2 * sx * sy, 2 * chans), BF16),
            pltpu.VMEM((2 * sx * sy, 2 * chans), BF16),
            dma(6), dma(6), *stream_refs,
        ],
        compiler_params=pltpu.CompilerParams(
            collective_id=0, has_side_effects=True, vmem_limit_bytes=40 * 1024 * 1024
        ),
    )(
        jnp.transpose(grad_out, (1, 2, 3, 0)),
        jnp.transpose(features, (1, 2, 3, 0)),
        brick_mask,
        voxel_mask,
        weight,
    )
    return jnp.transpose(grad_input, (3, 0, 1, 2)), grad_weight


def solution(mesh):
    sizes = tuple(mesh.shape[name] for name in ("gx", "gy", "gz"))
    return jax.shard_map(
        functools.partial(local, sizes),
        mesh=mesh,
        in_specs=(
            P(None, "gx", "gy", "gz"),
            P(None, "gx", "gy", "gz"),
            P("gx", "gy", "gz"),
            P("gx", "gy", "gz"),
            P(),
        ),
        out_specs=(P(None, "gx", "gy", "gz"), P()),
        check_vma=False,
    )
```

```python
import functools
import math

import jax
import jax.numpy as jnp
from jax import lax
from jax.experimental import pallas as pl
from jax.experimental.pallas import tpu as pltpu
from jax.sharding import PartitionSpec as P

BRICK = 8
MESH = pl.DeviceIdType.MESH
F32, BF16 = jnp.float32, jnp.bfloat16


def ceil_div(a, b):
    return -(-a // b)


def plan(sizes, chans):
    n_gx, n_gy, n_gz = sizes
    cores = 2 if n_gz % 2 == 0 else 1
    plane = n_gy * (n_gz // cores)
    tiles = 9 * chans * chans // 1024
    streams = []
    for count, order in ((tiles, (cores, n_gx, plane)), (2 * tiles, (cores, plane, n_gx))):
        stages, left = [], count
        for peers in order:
            left = ceil_div(left, peers)
            stages.append((peers, left))
        streams.append((count, stages))
    return cores, plane, streams


def div(x, n):
    return lax.shift_right_logical(x, n.bit_length() - 1) if n & (n - 1) == 0 else x // n


def mod(x, n):
    return x & (n - 1) if n & (n - 1) == 0 else lax.rem(x, n)


def iota(shape, dim):
    return lax.broadcasted_iota(jnp.int32, shape, dim)


def kernel(
    sizes, scale, g_hbm, f_hbm, b_hbm, v_hbm, w_hbm, gi_ref, gw_ref,
    g_ref, f_ref, b_ref, v_ref, w_ref, load_sem,
    pad, cols, mask, faces, rims, halo_send, halo_recv, *stream_refs,
):
    n_gx, n_gy, n_gz = sizes
    sx, sy, sz, chans = g_ref.shape
    nxy, count = sx * sy, sx * sy * sz
    cores, plane, streams = plan(sizes, chans)
    loads = [
        pltpu.make_async_copy(src, dst, load_sem.at[i])
        for i, (src, dst) in enumerate(
            [(b_hbm, b_ref), (v_hbm, v_ref), (g_hbm, g_ref), (f_hbm, f_ref), (w_hbm, w_ref)]
        )
    ]
    for load in loads:
        load.start()
    gx, gy, gz = lax.axis_index("gx"), lax.axis_index("gy"), lax.axis_index("gz")
    core, xh = lax.rem(gz, cores), gz // cores
    wide = n_gz // cores
    spot = gy * wide + xh

    def plane_peer(step):
        other = lax.rem(spot + step, plane)
        return (gx, other // wide, lax.rem(other, wide) * cores + core)

    def line_peer(step):
        return (lax.rem(gx + step, n_gx), gy, gz)

    def core_peer(step):
        return (gx, gy, xh * cores + lax.rem(core + step, cores))

    partners = [plane_peer(s) for s in range(1, plane)] + [line_peer(s) for s in range(1, n_gx)]
    if cores == 2:
        partners.append(core_peer(1))
    if n_gz > cores:
        partners.append((gx, gy, lax.rem(gz + n_gz + 2 * core - 1, n_gz)))
    barrier = pltpu.get_barrier_semaphore()
    for partner in partners:
        pl.semaphore_signal(barrier, inc=1, device_id=partner, device_id_type=MESH)

    bricks = jnp.zeros((sx, sy, sz), jnp.int32)
    loads[0].wait()
    loads[1].wait()
    at = [div(iota((sx, sy, sz), d), BRICK) for d in range(3)]
    for i in range(b_ref.shape[0]):
        for j in range(b_ref.shape[1]):
            for l in range(b_ref.shape[2]):
                here = (at[0] == i) & (at[1] == j) & (at[2] == l)
                bricks = jnp.where(here, b_ref[i, j, l], bricks)
    active = jnp.where(bricks * v_ref[...] > 0, 1.0, 0.0).reshape(nxy, sz).astype(BF16)
    own = jnp.where(div(iota((count, nxy), 0), sz) == iota((count, nxy), 1), 1.0, 0.0).astype(BF16)
    spread = jnp.dot(own, active, preferred_element_type=F32)
    level = mod(iota((count, sz), 0), sz) == iota((count, sz), 1)
    spread = jnp.where(level, spread, 0.0).astype(BF16)
    lit = jnp.dot(spread, jnp.ones((sz, chans), BF16), preferred_element_type=F32)
    mask[...] = lit
    lit = lit.astype(BF16)
    loads[2].wait()
    grad = g_ref[...].reshape(count, chans) * lit

    row, col = iota((2 * nxy, count), 0), iota((2 * nxy, count), 1)
    pick = jnp.where(row < nxy, row * sz, (row - nxy) * sz + sz - 1) == col
    pick = jnp.where(pick, 1.0, 0.0).astype(BF16)
    ends = jnp.dot(pick, grad, preferred_element_type=F32)
    zeros = jnp.zeros((2 * nxy, chans), F32)
    faces[...] = jnp.concatenate([zeros, ends], axis=1).astype(BF16)

    pl.semaphore_wait(barrier, len(partners))

    def swap(base, index, length, device, low_src, high_src, low_dst, high_dst):
        def down():
            return pltpu.make_async_remote_copy(
                src_ref=low_src, dst_ref=high_dst, send_sem=halo_send.at[base],
                recv_sem=halo_recv.at[base], device_id=device(lax.rem(index + length - 1, length)),
                device_id_type=MESH,
            )

        def up():
            return pltpu.make_async_remote_copy(
                src_ref=high_src, dst_ref=low_dst, send_sem=halo_send.at[base + 1],
                recv_sem=halo_recv.at[base + 1], device_id=device(lax.rem(index + 1, length)),
                device_id_type=MESH,
            )

        if length > 1:
            @pl.when(index > 0)
            def _():
                down().start()

            @pl.when(index < length - 1)
            def _():
                up().start()

        def finish():
            @pl.when(index == 0)
            def _():
                low_dst[...] = jnp.zeros(low_dst.shape, low_dst.dtype)

            @pl.when(index == length - 1)
            def _():
                high_dst[...] = jnp.zeros(high_dst.shape, high_dst.dtype)

            if length > 1:
                @pl.when(index > 0)
                def _():
                    up().wait_recv()
                    down().wait_send()

                @pl.when(index < length - 1)
                def _():
                    down().wait_recv()
                    up().wait_send()

        return finish

    def columns(tile):
        lead = tile.shape[:-2]
        rows = math.prod(tile.shape[:-1])
        wide_tile = tile.reshape(rows, 2 * chans).astype(F32)
        after = pltpu.roll(wide_tile, rows - 1, 0)
        before = pltpu.roll(wide_tile, 1, 0)
        other = pltpu.roll(wide_tile, chans, 1)
        z, lane = mod(iota(wide_tile.shape, 0), sz), iota(wide_tile.shape, 1)
        first = jnp.where((lane < chans) & (z != sz - 1), after, other)
        second = jnp.where(z == 0, other, before)
        both = jnp.concatenate([first, second], axis=1).astype(BF16)
        return both.reshape(*lead, sz, 4 * chans)

    finish = swap(
        0, gz, n_gz, lambda i: (gx, gy, i),
        faces.at[pl.ds(0, nxy)], faces.at[pl.ds(nxy, nxy)],
        rims.at[pl.ds(0, nxy)], rims.at[pl.ds(nxy, nxy)],
    )
    loads[3].wait()
    feat = (f_ref[...].reshape(count, chans) * lit).astype(F32).T.astype(BF16)
    finish()
    row, col = iota((count, 2 * nxy), 0), iota((count, 2 * nxy), 1)
    place = jnp.where(col < nxy, col * sz, (col - nxy) * sz + sz - 1) == row
    place = jnp.where(place, 1.0, 0.0).astype(BF16)
    rim = jnp.dot(place, rims[...], preferred_element_type=F32)
    body = jnp.concatenate([grad.astype(F32), jnp.zeros((count, chans), F32)], axis=1) + rim
    pad[1 : sx + 1, 1 : sy + 1] = body.astype(BF16).reshape(sx, sy, sz, 2 * chans)

    inner = pl.ds(1, sy)
    finish = swap(
        2, gx, n_gx, lambda i: (i, gy, gz),
        pad.at[1, inner], pad.at[sx, inner], pad.at[0, inner], pad.at[sx + 1, inner],
    )
    cols[1 : sx + 1, 1 : sy + 1] = columns(pad[1 : sx + 1, 1 : sy + 1])
    finish()
    finish = swap(
        4, gy, n_gy, lambda i: (gx, i, gz),
        pad.at[:, 1], pad.at[:, sy], pad.at[:, 0], pad.at[:, sy + 1],
    )
    cols[0, 1 : sy + 1] = columns(pad[0, 1 : sy + 1])
    cols[sx + 1, 1 : sy + 1] = columns(pad[sx + 1, 1 : sy + 1])

    half = chans // 2
    per = half // 8

    def shifted(a, b):
        return cols[1 - a : 1 - a + sx, 1 - b : 1 - b + sy].reshape(count, 4 * chans)

    def weight_term(a, b, terms, first):
        got = jnp.dot(feat, shifted(a, b), preferred_element_type=F32)
        low = iota((half, 2 * chans), 1) < chans
        for e in range(3):
            tile = e // 2
            top = got[:half, tile * 2 * chans : (tile + 1) * 2 * chans]
            end = got[half:, tile * 2 * chans : (tile + 1) * 2 * chans]
            if e % 2 == 0:
                both = jnp.where(low, top, pltpu.roll(end, chans, 1))
            else:
                both = jnp.where(low, pltpu.roll(top, chans, 1), end)
            at_tile = (first + e) * per
            terms[at_tile : at_tile + per] = both.reshape(per, 8, 2 * chans)

    class Stream:
        def __init__(self, which):
            self.tiles, self.stages = streams[which]
            refs = stream_refs[which * 15 : (which + 1) * 15]
            self.sums, self.ins, self.outs = refs[0:3], refs[3:6], refs[6:9]
            self.sends, self.recvs = refs[9:12], refs[12:15]
            across, along = (spot, plane_peer), (gx, line_peer)
            self.who = [(core, core_peer)] + ([along, across] if which == 0 else [across, along])
            self.flights = []

        def fly(self, level, slot, src, dst, step):
            copy = pltpu.make_async_remote_copy(
                src_ref=src, dst_ref=dst, send_sem=self.sends[level].at[slot],
                recv_sem=self.recvs[level].at[slot], device_id=self.who[level][1](step),
                device_id_type=MESH,
            )
            copy.start()
            self.flights.append(copy)

        def fill(self, level, used):
            peers, share = self.stages[level]
            if peers * share > used:
                self.sums[level][used:] = jnp.zeros((peers * share - used, 8, 2 * chans), F32)

        def give(self, level):
            peers, share = self.stages[level]
            for step in range(1, peers):
                other = lax.rem(self.who[level][0] + step, peers)
                self.fly(level, step - 1, self.sums[level].at[pl.ds(other * share, share)],
                         self.ins[level].at[step - 1], step)

        def take(self, level):
            peers, share = self.stages[level]
            acc = self.sums[level][pl.ds(self.who[level][0] * share, share)]
            for step, copy in enumerate(self.flights):
                copy.wait()
                acc = acc + self.ins[level][step]
            self.flights = []
            if level < 2:
                self.sums[level + 1][:share] = acc
                self.fill(level + 1, share)
            else:
                self.outs[2][pl.ds(self.who[2][0] * share, share)] = acc * scale

        def give_back(self, level):
            peers, share = self.stages[level]
            here = pl.ds(self.who[level][0] * share, share)
            src = self.outs[level].at[here] if level == 2 else self.outs[level + 1].at[pl.ds(0, share)]
            for step in range(1, peers):
                self.fly(level, peers + step - 2, src, self.outs[level].at[here], step)
            if level < 2:
                self.outs[level][here] = self.outs[level + 1][:share]

        def take_back(self):
            for copy in self.flights:
                copy.wait()
            self.flights = []

    early, late = Stream(0), Stream(1)
    for a in (-1, 0, 1):
        weight_term(a, 0, early.sums[0], 3 * (a + 1))
    early.fill(0, early.tiles)
    early.give(0)
    finish()
    cols[:, 0] = columns(pad[:, 0])
    cols[:, sy + 1] = columns(pad[:, sy + 1])
    for a in (-1, 0, 1):
        weight_term(a, -1, late.sums[0], 3 * (a + 1))
    early.take(0)
    early.give(1)
    for a in (-1, 0, 1):
        weight_term(a, 1, late.sums[0], 9 + 3 * (a + 1))
    late.fill(0, late.tiles)
    late.give(0)

    def input_rows(x):
        wide_cols, kernels = [], []
        for a in (-1, 0, 1):
            for b in (-1, 0, 1):
                rows = cols[x + 1 - a, 1 - b : 1 - b + sy].reshape(sy * sz, 4 * chans)
                k = 9 * (a + 1) + 3 * (b + 1)
                wide_cols.append(rows[:, : 3 * chans])
                kernels.append(w_ref[:, k * chans : (k + 3) * chans])
        total = jnp.zeros((sy * sz, chans), F32)
        for rows, kern in zip(wide_cols, kernels):
            total = total + lax.dot_general(
                rows, kern, (((1,), (1,)), ((), ())), preferred_element_type=F32
            )
        keep = mask[x * sy * sz : (x + 1) * sy * sz] > 0
        gi_ref[x] = jnp.where(keep, total, 0.0).astype(BF16).reshape(sy, sz, chans)

    loads[4].wait()
    late.take(0)
    late.give(1)
    for x in range(sx // 2):
        input_rows(x)
    early.take(1)
    early.give(2)
    for x in range(sx // 2, sx):
        input_rows(x)
    late.take(1)
    late.give(2)
    early.take(2)
    early.give_back(2)
    late.take(2)
    late.give_back(2)
    early.take_back()
    early.give_back(1)
    late.take_back()
    late.give_back(1)
    early.take_back()
    early.give_back(0)
    late.take_back()
    late.give_back(0)
    early.take_back()
    late.take_back()

    def block(k):
        a, b, e = k // 9, k // 3 % 3, k % 3
        full = early.outs[0] if b == 1 else late.outs[0]
        place = (0 if b < 2 else 9) + 3 * a + e
        return full[place * per : (place + 1) * per].reshape(half, 2 * chans)

    low = iota((half, 2 * chans), 1) < chans
    for k in range(0, 27, 2):
        one = block(k)
        if k == 26:
            gw_ref[:half, k * chans :] = one[:, :chans]
            gw_ref[half:, k * chans :] = pltpu.roll(one, chans, 1)[:, :chans]
            continue
        two = block(k + 1)
        at_k = slice(k * chans, (k + 2) * chans)
        gw_ref[:half, at_k] = jnp.where(low, one, pltpu.roll(two, chans, 1))
        gw_ref[half:, at_k] = jnp.where(low, pltpu.roll(one, chans, 1), two)


def local(sizes, grad_out, features, brick_mask, voxel_mask, weight):
    chans, sx, sy, sz = grad_out.shape
    n_gx, n_gy, n_gz = sizes
    cores, plane, streams = plan(sizes, chans)
    scale = 1.0 / math.sqrt(sx * sy * sz * n_gx * n_gy * n_gz)
    vmem = pl.BlockSpec(memory_space=pltpu.VMEM)
    dma = lambda n: pltpu.SemaphoreType.DMA((max(n, 1),))
    hbm = pl.BlockSpec(memory_space=pltpu.HBM)
    tile = (8, 2 * chans)
    stream_refs = []
    for _, stages in streams:
        whole = [pltpu.VMEM((peers * share, *tile), F32) for peers, share in stages]
        ins = [pltpu.VMEM((max(peers - 1, 1), share, *tile), F32) for peers, share in stages]
        sems = [dma(2 * (peers - 1)) for peers, _ in stages]
        stream_refs += whole + ins + whole + sems + sems
    grad_input, grad_weight = pl.pallas_call(
        functools.partial(kernel, sizes, scale),
        out_shape=(
            jax.ShapeDtypeStruct((sx, sy, sz, chans), BF16),
            jax.ShapeDtypeStruct((chans, 27 * chans), F32),
        ),
        in_specs=[hbm] * 5,
        out_specs=(vmem, vmem),
        scratch_shapes=[
            pltpu.VMEM((sx, sy, sz, chans), BF16),
            pltpu.VMEM((sx, sy, sz, chans), BF16),
            pltpu.SMEM(brick_mask.shape, jnp.int32),
            pltpu.VMEM((sx, sy, sz), jnp.int32),
            pltpu.VMEM(weight.shape, BF16),
            dma(5),
            pltpu.VMEM((sx + 2, sy + 2, sz, 2 * chans), BF16),
            pltpu.VMEM((sx + 2, sy + 2, sz, 4 * chans), BF16),
            pltpu.VMEM((sx * sy * sz, chans), F32),
            pltpu.VMEM((2 * sx * sy, 2 * chans), BF16),
            pltpu.VMEM((2 * sx * sy, 2 * chans), BF16),
            dma(6), dma(6), *stream_refs,
        ],
        compiler_params=pltpu.CompilerParams(
            collective_id=0, has_side_effects=True, vmem_limit_bytes=62 * 1024 * 1024
        ),
    )(
        jnp.transpose(grad_out, (1, 2, 3, 0)),
        jnp.transpose(features, (1, 2, 3, 0)),
        brick_mask,
        voxel_mask,
        weight,
    )
    return jnp.transpose(grad_input, (3, 0, 1, 2)), grad_weight


def solution(mesh):
    sizes = tuple(mesh.shape[name] for name in ("gx", "gy", "gz"))
    return jax.shard_map(
        functools.partial(local, sizes),
        mesh=mesh,
        in_specs=(
            P(None, "gx", "gy", "gz"),
            P(None, "gx", "gy", "gz"),
            P("gx", "gy", "gz"),
            P("gx", "gy", "gz"),
            P(),
        ),
        out_specs=(P(None, "gx", "gy", "gz"), P()),
        check_vma=False,
    )
```

```python
import functools
import math

import jax
import jax.numpy as jnp
from jax import lax
from jax.experimental import pallas as pl
from jax.experimental.pallas import tpu as pltpu
from jax.sharding import PartitionSpec as P

BRICK = 8
MESH = pl.DeviceIdType.MESH
F32, BF16 = jnp.float32, jnp.bfloat16


def ceil_div(a, b):
    return -(-a // b)


def plan(sizes, chans):
    n_gx, n_gy, n_gz = sizes
    plane = n_gy * n_gz
    tiles = 9 * chans * chans // 1024
    return plane, [(count, ceil_div(count, plane)) for count in (tiles, 2 * tiles)]


def div(x, n):
    return lax.shift_right_logical(x, n.bit_length() - 1) if n & (n - 1) == 0 else x // n


def mod(x, n):
    return x & (n - 1) if n & (n - 1) == 0 else lax.rem(x, n)


def iota(shape, dim):
    return lax.broadcasted_iota(jnp.int32, shape, dim)


def kernel(
    sizes, scale, g_hbm, f_hbm, b_hbm, v_hbm, w_hbm, gi_ref, gw_ref,
    g_ref, f_ref, b_ref, v_ref, w_ref, load_sem,
    pad, cols, mask, faces, rims, halo_send, halo_recv, *stream_refs,
):
    n_gx, n_gy, n_gz = sizes
    sx, sy, sz, chans = g_ref.shape
    nxy, count = sx * sy, sx * sy * sz
    plane, streams = plan(sizes, chans)
    loads = [
        pltpu.make_async_copy(src, dst, load_sem.at[i])
        for i, (src, dst) in enumerate(
            [(b_hbm, b_ref), (v_hbm, v_ref), (g_hbm, g_ref), (f_hbm, f_ref), (w_hbm, w_ref)]
        )
    ]
    for load in loads:
        load.start()
    gx, gy, gz = lax.axis_index("gx"), lax.axis_index("gy"), lax.axis_index("gz")
    spot = gy * n_gz + gz

    def plane_peer(step):
        other = lax.rem(spot + step, plane)
        return (gx, other // n_gz, lax.rem(other, n_gz))

    def line_peer(step):
        return (lax.rem(gx + step, n_gx), gy, gz)

    partners = [plane_peer(s) for s in range(1, plane)] + [line_peer(s) for s in range(1, n_gx)]
    barrier = pltpu.get_barrier_semaphore()
    for partner in partners:
        pl.semaphore_signal(barrier, inc=1, device_id=partner, device_id_type=MESH)

    bricks = jnp.zeros((sx, sy, sz), jnp.int32)
    loads[0].wait()
    loads[1].wait()
    at = [div(iota((sx, sy, sz), d), BRICK) for d in range(3)]
    for i in range(b_ref.shape[0]):
        for j in range(b_ref.shape[1]):
            for l in range(b_ref.shape[2]):
                here = (at[0] == i) & (at[1] == j) & (at[2] == l)
                bricks = jnp.where(here, b_ref[i, j, l], bricks)
    active = jnp.where(bricks * v_ref[...] > 0, 1.0, 0.0).reshape(nxy, sz).astype(BF16)
    own = jnp.where(div(iota((count, nxy), 0), sz) == iota((count, nxy), 1), 1.0, 0.0).astype(BF16)
    spread = jnp.dot(own, active, preferred_element_type=F32)
    level = mod(iota((count, sz), 0), sz) == iota((count, sz), 1)
    spread = jnp.where(level, spread, 0.0).astype(BF16)
    lit = jnp.dot(spread, jnp.ones((sz, chans), BF16), preferred_element_type=F32)
    mask[...] = lit
    lit = lit.astype(BF16)
    loads[2].wait()
    grad = g_ref[...].reshape(count, chans) * lit

    row, col = iota((2 * nxy, count), 0), iota((2 * nxy, count), 1)
    pick = jnp.where(row < nxy, row * sz, (row - nxy) * sz + sz - 1) == col
    pick = jnp.where(pick, 1.0, 0.0).astype(BF16)
    ends = jnp.dot(pick, grad, preferred_element_type=F32)
    zeros = jnp.zeros((2 * nxy, chans), F32)
    faces[...] = jnp.concatenate([zeros, ends], axis=1).astype(BF16)

    pl.semaphore_wait(barrier, len(partners))

    def swap(base, index, length, device, low_src, high_src, low_dst, high_dst):
        def down():
            return pltpu.make_async_remote_copy(
                src_ref=low_src, dst_ref=high_dst, send_sem=halo_send.at[base],
                recv_sem=halo_recv.at[base], device_id=device(lax.rem(index + length - 1, length)),
                device_id_type=MESH,
            )

        def up():
            return pltpu.make_async_remote_copy(
                src_ref=high_src, dst_ref=low_dst, send_sem=halo_send.at[base + 1],
                recv_sem=halo_recv.at[base + 1], device_id=device(lax.rem(index + 1, length)),
                device_id_type=MESH,
            )

        if length > 1:
            @pl.when(index > 0)
            def _():
                down().start()

            @pl.when(index < length - 1)
            def _():
                up().start()

        def finish():
            @pl.when(index == 0)
            def _():
                low_dst[...] = jnp.zeros(low_dst.shape, low_dst.dtype)

            @pl.when(index == length - 1)
            def _():
                high_dst[...] = jnp.zeros(high_dst.shape, high_dst.dtype)

            if length > 1:
                @pl.when(index > 0)
                def _():
                    up().wait_recv()
                    down().wait_send()

                @pl.when(index < length - 1)
                def _():
                    down().wait_recv()
                    up().wait_send()

        return finish

    def columns(tile):
        lead = tile.shape[:-2]
        rows = math.prod(tile.shape[:-1])
        wide_tile = tile.reshape(rows, 2 * chans).astype(F32)
        after = pltpu.roll(wide_tile, rows - 1, 0)
        before = pltpu.roll(wide_tile, 1, 0)
        other = pltpu.roll(wide_tile, chans, 1)
        z, lane = mod(iota(wide_tile.shape, 0), sz), iota(wide_tile.shape, 1)
        first = jnp.where((lane < chans) & (z != sz - 1), after, other)
        second = jnp.where(z == 0, other, before)
        both = jnp.concatenate([first, second], axis=1).astype(BF16)
        return both.reshape(*lead, sz, 4 * chans)

    finish = swap(
        0, gz, n_gz, lambda i: (gx, gy, i),
        faces.at[pl.ds(0, nxy)], faces.at[pl.ds(nxy, nxy)],
        rims.at[pl.ds(0, nxy)], rims.at[pl.ds(nxy, nxy)],
    )
    loads[3].wait()
    feat = (f_ref[...].reshape(count, chans) * lit).astype(F32).T.astype(BF16)
    finish()
    row, col = iota((count, 2 * nxy), 0), iota((count, 2 * nxy), 1)
    place = jnp.where(col < nxy, col * sz, (col - nxy) * sz + sz - 1) == row
    place = jnp.where(place, 1.0, 0.0).astype(BF16)
    rim = jnp.dot(place, rims[...], preferred_element_type=F32)
    body = jnp.concatenate([grad.astype(F32), jnp.zeros((count, chans), F32)], axis=1) + rim
    pad[1 : sx + 1, 1 : sy + 1] = body.astype(BF16).reshape(sx, sy, sz, 2 * chans)

    inner = pl.ds(1, sy)
    finish = swap(
        2, gx, n_gx, lambda i: (i, gy, gz),
        pad.at[1, inner], pad.at[sx, inner], pad.at[0, inner], pad.at[sx + 1, inner],
    )
    cols[1 : sx + 1, 1 : sy + 1] = columns(pad[1 : sx + 1, 1 : sy + 1])
    finish()
    finish = swap(
        4, gy, n_gy, lambda i: (gx, i, gz),
        pad.at[:, 1], pad.at[:, sy], pad.at[:, 0], pad.at[:, sy + 1],
    )
    cols[0, 1 : sy + 1] = columns(pad[0, 1 : sy + 1])
    cols[sx + 1, 1 : sy + 1] = columns(pad[sx + 1, 1 : sy + 1])

    half = chans // 2
    per = half // 8

    def shifted(a, b):
        return cols[1 - a : 1 - a + sx, 1 - b : 1 - b + sy].reshape(count, 4 * chans)

    def weight_term(a, b, terms, first):
        got = jnp.dot(feat, shifted(a, b), preferred_element_type=F32)
        low = iota((half, 2 * chans), 1) < chans
        for e in range(3):
            tile = e // 2
            top = got[:half, tile * 2 * chans : (tile + 1) * 2 * chans]
            end = got[half:, tile * 2 * chans : (tile + 1) * 2 * chans]
            if e % 2 == 0:
                both = jnp.where(low, top, pltpu.roll(end, chans, 1))
            else:
                both = jnp.where(low, pltpu.roll(top, chans, 1), end)
            at_tile = (first + e) * per
            terms[at_tile : at_tile + per] = both.reshape(per, 8, 2 * chans)

    class Stream:
        def __init__(self, which):
            self.tiles, self.share = streams[which]
            refs = stream_refs[which * 10 : (which + 1) * 10]
            self.terms, self.got, self.line, self.out = refs[:4]
            self.sems = refs[4:]
            self.flights = []

        def fly(self, stage, slot, src, dst, device):
            copy = pltpu.make_async_remote_copy(
                src_ref=src, dst_ref=dst, send_sem=self.sems[2 * stage].at[slot],
                recv_sem=self.sems[2 * stage + 1].at[slot], device_id=device,
                device_id_type=MESH,
            )
            copy.start()
            self.flights.append(copy)

        def scatter(self):
            if plane * self.share > self.tiles:
                rest = plane * self.share - self.tiles
                self.terms[self.tiles :] = jnp.zeros((rest, 8, 2 * chans), F32)
            for step in range(1, plane):
                other = lax.rem(spot + step, plane)
                self.fly(0, step - 1, self.terms.at[pl.ds(other * self.share, self.share)],
                         self.got.at[step - 1], plane_peer(step))

        def exchange(self):
            acc = self.terms[pl.ds(spot * self.share, self.share)]
            for step, copy in enumerate(self.flights):
                copy.wait()
                acc = acc + self.got[step]
            self.flights = []
            self.line[gx] = acc
            for step in range(1, n_gx):
                self.fly(1, step - 1, self.line.at[gx], self.line.at[gx], line_peer(step))

        def gather(self):
            for copy in self.flights:
                copy.wait()
            self.flights = []
            acc = self.line[0]
            for i in range(1, n_gx):
                acc = acc + self.line[i]
            here = pl.ds(spot * self.share, self.share)
            self.out[here] = acc * scale
            for step in range(1, plane):
                self.fly(2, step - 1, self.out.at[here], self.out.at[here], plane_peer(step))

        def land(self):
            for copy in self.flights:
                copy.wait()

    early, late = Stream(0), Stream(1)
    for a in (-1, 0, 1):
        weight_term(a, 0, early.terms, 3 * (a + 1))
    early.scatter()
    finish()
    cols[:, 0] = columns(pad[:, 0])
    cols[:, sy + 1] = columns(pad[:, sy + 1])
    for a in (-1, 0, 1):
        weight_term(a, -1, late.terms, 3 * (a + 1))
    for a in (-1, 0, 1):
        weight_term(a, 1, late.terms, 9 + 3 * (a + 1))
    late.scatter()

    def input_rows(x):
        wide_cols, kernels = [], []
        for a in (-1, 0, 1):
            for b in (-1, 0, 1):
                rows = cols[x + 1 - a, 1 - b : 1 - b + sy].reshape(sy * sz, 4 * chans)
                k = 9 * (a + 1) + 3 * (b + 1)
                wide_cols.append(rows[:, : 3 * chans])
                kernels.append(w_ref[:, k * chans : (k + 3) * chans])
        total = jnp.zeros((sy * sz, chans), F32)
        for rows, kern in zip(wide_cols, kernels):
            total = total + lax.dot_general(
                rows, kern, (((1,), (1,)), ((), ())), preferred_element_type=F32
            )
        keep = mask[x * sy * sz : (x + 1) * sy * sz] > 0
        gi_ref[x] = jnp.where(keep, total, 0.0).astype(BF16).reshape(sy, sz, chans)

    loads[4].wait()
    early.exchange()
    for x in range(sx // 2):
        input_rows(x)
    late.exchange()
    for x in range(sx // 2, sx):
        input_rows(x)
    early.gather()
    late.gather()
    early.land()
    late.land()

    def block(k):
        a, b, e = k // 9, k // 3 % 3, k % 3
        full = early.out if b == 1 else late.out
        place = (0 if b < 2 else 9) + 3 * a + e
        return full[place * per : (place + 1) * per].reshape(half, 2 * chans)

    low = iota((half, 2 * chans), 1) < chans
    for k in range(0, 27, 2):
        one = block(k)
        if k == 26:
            gw_ref[:half, k * chans :] = one[:, :chans]
            gw_ref[half:, k * chans :] = pltpu.roll(one, chans, 1)[:, :chans]
            continue
        two = block(k + 1)
        at_k = slice(k * chans, (k + 2) * chans)
        gw_ref[:half, at_k] = jnp.where(low, one, pltpu.roll(two, chans, 1))
        gw_ref[half:, at_k] = jnp.where(low, pltpu.roll(one, chans, 1), two)


def local(sizes, grad_out, features, brick_mask, voxel_mask, weight):
    chans, sx, sy, sz = grad_out.shape
    n_gx, n_gy, n_gz = sizes
    plane, streams = plan(sizes, chans)
    scale = 1.0 / math.sqrt(sx * sy * sz * n_gx * n_gy * n_gz)
    vmem = pl.BlockSpec(memory_space=pltpu.VMEM)
    dma = lambda n: pltpu.SemaphoreType.DMA((max(n, 1),))
    hbm = pl.BlockSpec(memory_space=pltpu.HBM)
    tile = (8, 2 * chans)
    stream_refs = []
    for _, share in streams:
        stream_refs += [
            pltpu.VMEM((plane * share, *tile), F32),
            pltpu.VMEM((max(plane - 1, 1), share, *tile), F32),
            pltpu.VMEM((n_gx, share, *tile), F32),
            pltpu.VMEM((plane * share, *tile), F32),
        ]
        stream_refs += [dma(n - 1) for n in (plane, plane, n_gx, n_gx, plane, plane)]
    grad_input, grad_weight = pl.pallas_call(
        functools.partial(kernel, sizes, scale),
        out_shape=(
            jax.ShapeDtypeStruct((sx, sy, sz, chans), BF16),
            jax.ShapeDtypeStruct((chans, 27 * chans), F32),
        ),
        in_specs=[hbm] * 5,
        out_specs=(vmem, vmem),
        scratch_shapes=[
            pltpu.VMEM((sx, sy, sz, chans), BF16),
            pltpu.VMEM((sx, sy, sz, chans), BF16),
            pltpu.SMEM(brick_mask.shape, jnp.int32),
            pltpu.VMEM((sx, sy, sz), jnp.int32),
            pltpu.VMEM(weight.shape, BF16),
            dma(5),
            pltpu.VMEM((sx + 2, sy + 2, sz, 2 * chans), BF16),
            pltpu.VMEM((sx + 2, sy + 2, sz, 4 * chans), BF16),
            pltpu.VMEM((sx * sy * sz, chans), F32),
            pltpu.VMEM((2 * sx * sy, 2 * chans), BF16),
            pltpu.VMEM((2 * sx * sy, 2 * chans), BF16),
            dma(6), dma(6), *stream_refs,
        ],
        compiler_params=pltpu.CompilerParams(
            collective_id=0, has_side_effects=True, vmem_limit_bytes=62 * 1024 * 1024
        ),
    )(
        jnp.transpose(grad_out, (1, 2, 3, 0)),
        jnp.transpose(features, (1, 2, 3, 0)),
        brick_mask,
        voxel_mask,
        weight,
    )
    return jnp.transpose(grad_input, (3, 0, 1, 2)), grad_weight


def solution(mesh):
    sizes = tuple(mesh.shape[name] for name in ("gx", "gy", "gz"))
    return jax.shard_map(
        functools.partial(local, sizes),
        mesh=mesh,
        in_specs=(
            P(None, "gx", "gy", "gz"),
            P(None, "gx", "gy", "gz"),
            P("gx", "gy", "gz"),
            P("gx", "gy", "gz"),
            P(),
        ),
        out_specs=(P(None, "gx", "gy", "gz"), P()),
        check_vma=False,
    )
```

```python
import functools
import math

import jax
import jax.numpy as jnp
from jax import lax
from jax.experimental import pallas as pl
from jax.experimental.pallas import tpu as pltpu
from jax.sharding import PartitionSpec as P

BRICK = 8
MESH = pl.DeviceIdType.MESH
F32, BF16 = jnp.float32, jnp.bfloat16


def ceil_div(a, b):
    return -(-a // b)


def plan(sizes, chans):
    n_gx, n_gy, n_gz = sizes
    plane = n_gy * n_gz
    tiles = 9 * chans * chans // 1024
    return plane, [(count, ceil_div(count, plane)) for count in (tiles, 2 * tiles)]


def div(x, n):
    return lax.shift_right_logical(x, n.bit_length() - 1) if n & (n - 1) == 0 else x // n


def mod(x, n):
    return x & (n - 1) if n & (n - 1) == 0 else lax.rem(x, n)


def iota(shape, dim):
    return lax.broadcasted_iota(jnp.int32, shape, dim)


def kernel(
    sizes, scale, g_hbm, f_hbm, b_hbm, v_hbm, w_hbm, gi_ref, gw_ref,
    g_ref, f_ref, b_ref, v_ref, w_ref, load_sem,
    pad, cols, mask, faces, rims, halo_send, halo_recv, *stream_refs,
):
    n_gx, n_gy, n_gz = sizes
    sx, sy, sz, chans = g_ref.shape
    nxy, count = sx * sy, sx * sy * sz
    plane, streams = plan(sizes, chans)
    loads = [
        pltpu.make_async_copy(src, dst, load_sem.at[i])
        for i, (src, dst) in enumerate(
            [(b_hbm, b_ref), (v_hbm, v_ref), (g_hbm, g_ref), (f_hbm, f_ref), (w_hbm, w_ref)]
        )
    ]
    for load in loads:
        load.start()
    gx, gy, gz = lax.axis_index("gx"), lax.axis_index("gy"), lax.axis_index("gz")
    spot = gy * n_gz + gz

    def plane_peer(step):
        other = lax.rem(spot + step, plane)
        return (gx, other // n_gz, lax.rem(other, n_gz))

    def line_peer(step):
        return (lax.rem(gx + step, n_gx), gy, gz)

    partners = [plane_peer(s) for s in range(1, plane)] + [line_peer(s) for s in range(1, n_gx)]
    diagonals = [(dx, dy) for dx in (-1, 1) for dy in (-1, 1)]

    def corner_peer(dx, dy):
        return (lax.rem(gx + n_gx + dx, n_gx), lax.rem(gy + n_gy + dy, n_gy), gz)

    partners += [corner_peer(dx, dy) for dx, dy in diagonals]
    barrier = pltpu.get_barrier_semaphore()
    for partner in partners:
        pl.semaphore_signal(barrier, inc=1, device_id=partner, device_id_type=MESH)

    bricks = jnp.zeros((sx, sy, sz), jnp.int32)
    loads[0].wait()
    loads[1].wait()
    at = [div(iota((sx, sy, sz), d), BRICK) for d in range(3)]
    for i in range(b_ref.shape[0]):
        for j in range(b_ref.shape[1]):
            for l in range(b_ref.shape[2]):
                here = (at[0] == i) & (at[1] == j) & (at[2] == l)
                bricks = jnp.where(here, b_ref[i, j, l], bricks)
    active = jnp.where(bricks * v_ref[...] > 0, 1.0, 0.0).reshape(nxy, sz).astype(BF16)
    own = jnp.where(div(iota((count, nxy), 0), sz) == iota((count, nxy), 1), 1.0, 0.0).astype(BF16)
    spread = jnp.dot(own, active, preferred_element_type=F32)
    level = mod(iota((count, sz), 0), sz) == iota((count, sz), 1)
    spread = jnp.where(level, spread, 0.0).astype(BF16)
    lit = jnp.dot(spread, jnp.ones((sz, chans), BF16), preferred_element_type=F32)
    mask[...] = lit
    lit = lit.astype(BF16)
    loads[2].wait()
    grad = g_ref[...].reshape(count, chans) * lit

    row, col = iota((2 * nxy, count), 0), iota((2 * nxy, count), 1)
    pick = jnp.where(row < nxy, row * sz, (row - nxy) * sz + sz - 1) == col
    pick = jnp.where(pick, 1.0, 0.0).astype(BF16)
    ends = jnp.dot(pick, grad, preferred_element_type=F32)
    zeros = jnp.zeros((2 * nxy, chans), F32)
    faces[...] = jnp.concatenate([zeros, ends], axis=1).astype(BF16)

    pl.semaphore_wait(barrier, len(partners))

    def swap(base, index, length, device, low_src, high_src, low_dst, high_dst):
        def down():
            return pltpu.make_async_remote_copy(
                src_ref=low_src, dst_ref=high_dst, send_sem=halo_send.at[base],
                recv_sem=halo_recv.at[base], device_id=device(lax.rem(index + length - 1, length)),
                device_id_type=MESH,
            )

        def up():
            return pltpu.make_async_remote_copy(
                src_ref=high_src, dst_ref=low_dst, send_sem=halo_send.at[base + 1],
                recv_sem=halo_recv.at[base + 1], device_id=device(lax.rem(index + 1, length)),
                device_id_type=MESH,
            )

        if length > 1:
            @pl.when(index > 0)
            def _():
                down().start()

            @pl.when(index < length - 1)
            def _():
                up().start()

        def finish():
            @pl.when(index == 0)
            def _():
                low_dst[...] = jnp.zeros(low_dst.shape, low_dst.dtype)

            @pl.when(index == length - 1)
            def _():
                high_dst[...] = jnp.zeros(high_dst.shape, high_dst.dtype)

            if length > 1:
                @pl.when(index > 0)
                def _():
                    up().wait_recv()
                    down().wait_send()

                @pl.when(index < length - 1)
                def _():
                    down().wait_recv()
                    up().wait_send()

        return finish

    def columns(tile):
        lead = tile.shape[:-2]
        rows = math.prod(tile.shape[:-1])
        wide_tile = tile.reshape(rows, 2 * chans).astype(F32)
        after = pltpu.roll(wide_tile, rows - 1, 0)
        before = pltpu.roll(wide_tile, 1, 0)
        other = pltpu.roll(wide_tile, chans, 1)
        z, lane = mod(iota(wide_tile.shape, 0), sz), iota(wide_tile.shape, 1)
        first = jnp.where((lane < chans) & (z != sz - 1), after, other)
        second = jnp.where(z == 0, other, before)
        both = jnp.concatenate([first, second], axis=1).astype(BF16)
        return both.reshape(*lead, sz, 4 * chans)

    finish = swap(
        0, gz, n_gz, lambda i: (gx, gy, i),
        faces.at[pl.ds(0, nxy)], faces.at[pl.ds(nxy, nxy)],
        rims.at[pl.ds(0, nxy)], rims.at[pl.ds(nxy, nxy)],
    )
    loads[3].wait()
    feat = (f_ref[...].reshape(count, chans) * lit).astype(F32).T.astype(BF16)
    finish()
    row, col = iota((count, 2 * nxy), 0), iota((count, 2 * nxy), 1)
    place = jnp.where(col < nxy, col * sz, (col - nxy) * sz + sz - 1) == row
    place = jnp.where(place, 1.0, 0.0).astype(BF16)
    rim = jnp.dot(place, rims[...], preferred_element_type=F32)
    body = jnp.concatenate([grad.astype(F32), jnp.zeros((count, chans), F32)], axis=1) + rim
    pad[1 : sx + 1, 1 : sy + 1] = body.astype(BF16).reshape(sx, sy, sz, 2 * chans)

    inner = pl.ds(1, sy)
    finish = swap(
        2, gx, n_gx, lambda i: (i, gy, gz),
        pad.at[1, inner], pad.at[sx, inner], pad.at[0, inner], pad.at[sx + 1, inner],
    )
    along_x = pl.ds(1, sx)
    finish_y = swap(
        4, gy, n_gy, lambda i: (gx, i, gz),
        pad.at[along_x, 1], pad.at[along_x, sy], pad.at[along_x, 0], pad.at[along_x, sy + 1],
    )

    def corner(slot, dx, dy):
        src = pad.at[sx if dx > 0 else 1, sy if dy > 0 else 1]
        dst = pad.at[0 if dx > 0 else sx + 1, 0 if dy > 0 else sy + 1]
        copy = lambda: pltpu.make_async_remote_copy(
            src_ref=src, dst_ref=dst, send_sem=halo_send.at[6 + slot],
            recv_sem=halo_recv.at[6 + slot], device_id=corner_peer(dx, dy), device_id_type=MESH,
        )

        def inside(sign):
            x, y = gx + sign * dx, gy + sign * dy
            return (x >= 0) & (x < n_gx) & (y >= 0) & (y < n_gy)

        @pl.when(inside(1))
        def _():
            copy().start()

        def finish_corner():
            @pl.when(inside(-1))
            def _():
                copy().wait_recv()

            @pl.when(jnp.logical_not(inside(-1)))
            def _():
                dst[...] = jnp.zeros(dst.shape, dst.dtype)

            @pl.when(inside(1))
            def _():
                copy().wait_send()

        return finish_corner

    corners = [corner(slot, dx, dy) for slot, (dx, dy) in enumerate(diagonals)]
    cols[1 : sx + 1, 1 : sy + 1] = columns(pad[1 : sx + 1, 1 : sy + 1])
    finish()
    cols[0, 1 : sy + 1] = columns(pad[0, 1 : sy + 1])
    cols[sx + 1, 1 : sy + 1] = columns(pad[sx + 1, 1 : sy + 1])

    half = chans // 2
    per = half // 8

    def shifted(a, b):
        return cols[1 - a : 1 - a + sx, 1 - b : 1 - b + sy].reshape(count, 4 * chans)

    def weight_term(a, b, terms, first):
        got = jnp.dot(feat, shifted(a, b), preferred_element_type=F32)
        low = iota((half, 2 * chans), 1) < chans
        for e in range(3):
            tile = e // 2
            top = got[:half, tile * 2 * chans : (tile + 1) * 2 * chans]
            end = got[half:, tile * 2 * chans : (tile + 1) * 2 * chans]
            if e % 2 == 0:
                both = jnp.where(low, top, pltpu.roll(end, chans, 1))
            else:
                both = jnp.where(low, pltpu.roll(top, chans, 1), end)
            at_tile = (first + e) * per
            terms[at_tile : at_tile + per] = both.reshape(per, 8, 2 * chans)

    class Stream:
        def __init__(self, which):
            self.tiles, self.share = streams[which]
            refs = stream_refs[which * 10 : (which + 1) * 10]
            self.terms, self.got, self.line, self.out = refs[:4]
            self.sems = refs[4:]
            self.flights = []

        def fly(self, stage, slot, src, dst, device):
            copy = pltpu.make_async_remote_copy(
                src_ref=src, dst_ref=dst, send_sem=self.sems[2 * stage].at[slot],
                recv_sem=self.sems[2 * stage + 1].at[slot], device_id=device,
                device_id_type=MESH,
            )
            copy.start()
            self.flights.append(copy)

        def scatter(self):
            if plane * self.share > self.tiles:
                rest = plane * self.share - self.tiles
                self.terms[self.tiles :] = jnp.zeros((rest, 8, 2 * chans), F32)
            for step in range(1, plane):
                other = lax.rem(spot + step, plane)
                self.fly(0, step - 1, self.terms.at[pl.ds(other * self.share, self.share)],
                         self.got.at[step - 1], plane_peer(step))

        def exchange(self):
            acc = self.terms[pl.ds(spot * self.share, self.share)]
            for step, copy in enumerate(self.flights):
                copy.wait()
                acc = acc + self.got[step]
            self.flights = []
            self.line[gx] = acc
            for step in range(1, n_gx):
                self.fly(1, step - 1, self.line.at[gx], self.line.at[gx], line_peer(step))

        def gather(self):
            for copy in self.flights:
                copy.wait()
            self.flights = []
            acc = self.line[0]
            for i in range(1, n_gx):
                acc = acc + self.line[i]
            here = pl.ds(spot * self.share, self.share)
            self.out[here] = acc * scale
            for step in range(1, plane):
                self.fly(2, step - 1, self.out.at[here], self.out.at[here], plane_peer(step))

        def land(self):
            for copy in self.flights:
                copy.wait()

    early, late = Stream(0), Stream(1)
    for a in (-1, 0, 1):
        weight_term(a, 0, early.terms, 3 * (a + 1))
    early.scatter()
    finish_y()
    for finish_corner in corners:
        finish_corner()
    cols[:, 0] = columns(pad[:, 0])
    cols[:, sy + 1] = columns(pad[:, sy + 1])
    for a in (-1, 0, 1):
        weight_term(a, -1, late.terms, 3 * (a + 1))
    for a in (-1, 0, 1):
        weight_term(a, 1, late.terms, 9 + 3 * (a + 1))
    late.scatter()

    def input_rows(x):
        wide_cols, kernels = [], []
        for a in (-1, 0, 1):
            for b in (-1, 0, 1):
                rows = cols[x + 1 - a, 1 - b : 1 - b + sy].reshape(sy * sz, 4 * chans)
                k = 9 * (a + 1) + 3 * (b + 1)
                wide_cols.append(rows[:, : 3 * chans])
                kernels.append(w_ref[:, k * chans : (k + 3) * chans])
        total = jnp.zeros((sy * sz, chans), F32)
        for rows, kern in zip(wide_cols, kernels):
            total = total + lax.dot_general(
                rows, kern, (((1,), (1,)), ((), ())), preferred_element_type=F32
            )
        keep = mask[x * sy * sz : (x + 1) * sy * sz] > 0
        gi_ref[x] = jnp.where(keep, total, 0.0).astype(BF16).reshape(sy, sz, chans)

    loads[4].wait()
    early.exchange()
    for x in range(sx // 2):
        input_rows(x)
    late.exchange()
    for x in range(sx // 2, sx):
        input_rows(x)
    early.gather()
    late.gather()
    early.land()
    late.land()

    def block(k):
        a, b, e = k // 9, k // 3 % 3, k % 3
        full = early.out if b == 1 else late.out
        place = (0 if b < 2 else 9) + 3 * a + e
        return full[place * per : (place + 1) * per].reshape(half, 2 * chans)

    low = iota((half, 2 * chans), 1) < chans
    for k in range(0, 27, 2):
        one = block(k)
        if k == 26:
            gw_ref[:half, k * chans :] = one[:, :chans]
            gw_ref[half:, k * chans :] = pltpu.roll(one, chans, 1)[:, :chans]
            continue
        two = block(k + 1)
        at_k = slice(k * chans, (k + 2) * chans)
        gw_ref[:half, at_k] = jnp.where(low, one, pltpu.roll(two, chans, 1))
        gw_ref[half:, at_k] = jnp.where(low, pltpu.roll(one, chans, 1), two)


def local(sizes, grad_out, features, brick_mask, voxel_mask, weight):
    chans, sx, sy, sz = grad_out.shape
    n_gx, n_gy, n_gz = sizes
    plane, streams = plan(sizes, chans)
    scale = 1.0 / math.sqrt(sx * sy * sz * n_gx * n_gy * n_gz)
    vmem = pl.BlockSpec(memory_space=pltpu.VMEM)
    dma = lambda n: pltpu.SemaphoreType.DMA((max(n, 1),))
    hbm = pl.BlockSpec(memory_space=pltpu.HBM)
    tile = (8, 2 * chans)
    stream_refs = []
    for _, share in streams:
        stream_refs += [
            pltpu.VMEM((plane * share, *tile), F32),
            pltpu.VMEM((max(plane - 1, 1), share, *tile), F32),
            pltpu.VMEM((n_gx, share, *tile), F32),
            pltpu.VMEM((plane * share, *tile), F32),
        ]
        stream_refs += [dma(n - 1) for n in (plane, plane, n_gx, n_gx, plane, plane)]
    grad_input, grad_weight = pl.pallas_call(
        functools.partial(kernel, sizes, scale),
        out_shape=(
            pltpu.VMEM((sx, sy, sz, chans), BF16),
            pltpu.VMEM((chans, 27 * chans), F32),
        ),
        in_specs=[hbm] * 5,
        out_specs=(vmem, vmem),
        scratch_shapes=[
            pltpu.VMEM((sx, sy, sz, chans), BF16),
            pltpu.VMEM((sx, sy, sz, chans), BF16),
            pltpu.SMEM(brick_mask.shape, jnp.int32),
            pltpu.VMEM((sx, sy, sz), jnp.int32),
            pltpu.VMEM(weight.shape, BF16),
            dma(5),
            pltpu.VMEM((sx + 2, sy + 2, sz, 2 * chans), BF16),
            pltpu.VMEM((sx + 2, sy + 2, sz, 4 * chans), BF16),
            pltpu.VMEM((sx * sy * sz, chans), F32),
            pltpu.VMEM((2 * sx * sy, 2 * chans), BF16),
            pltpu.VMEM((2 * sx * sy, 2 * chans), BF16),
            dma(10), dma(10), *stream_refs,
        ],
        compiler_params=pltpu.CompilerParams(
            collective_id=0, has_side_effects=True, vmem_limit_bytes=60 * 1024 * 1024
        ),
    )(
        jnp.transpose(grad_out, (1, 2, 3, 0)),
        jnp.transpose(features, (1, 2, 3, 0)),
        brick_mask,
        voxel_mask,
        weight,
    )
    return jnp.transpose(grad_input, (3, 0, 1, 2)), grad_weight


def solution(mesh):
    sizes = tuple(mesh.shape[name] for name in ("gx", "gy", "gz"))
    return jax.shard_map(
        functools.partial(local, sizes),
        mesh=mesh,
        in_specs=(
            P(None, "gx", "gy", "gz"),
            P(None, "gx", "gy", "gz"),
            P("gx", "gy", "gz"),
            P("gx", "gy", "gz"),
            P(),
        ),
        out_specs=(P(None, "gx", "gy", "gz"), P()),
        check_vma=False,
    )
```
